128 devices in a mesh: expert: 32 (over z, x, core), dp: 4 (over y).
Axes of the slice: x: 4, y: 4, z: 4, core: 2. Of those that a mesh axis runs over, the one named last changes fastest.
Arguments:
- tokens: bfloat16 [16384, 2048], P(('expert', 'dp')), may hold values from -6 to 6
- expert_ids: int32 [16384, 8], P(('expert', 'dp')), may hold values from 0 to 31, all different within a row
- combine_weights: float32 [16384, 8], P(('expert', 'dp')), may hold values from 0.05 to 0.5
- grad_output: bfloat16 [16384, 2048], P(('expert', 'dp')), may hold values from -6 to 6
- swap_flags: int32 [32], replicated, may hold values from 0 to 1, as said below
- w_gate: bfloat16 [32, 2048, 768], P('expert'), may hold values from -0.125 to 0.125
- w_up: bfloat16 [32, 2048, 768], P('expert'), may hold values from -0.125 to 0.125
- w_down: bfloat16 [32, 768, 2048], P('expert'), may hold values from -0.21875 to 0.21875
Outputs:
- mixed: bfloat16 [16384, 2048], P(('expert', 'dp'))
- grad_tokens: bfloat16 [16384, 2048], P(('expert', 'dp'))
- grad_weights: float32 [16384, 8], P(('expert', 'dp'))
- grad_gate: float32 [32, 2048, 768], P('expert', 'dp')
- grad_up: float32 [32, 2048, 768], P('expert', 'dp')
- grad_down: float32 [32, 768, 2048], P('expert', None, 'dp')
The draws below stay inside these ranges and needn't reach their ends.
Inputs may be any that keep to these rules, and one draw needn't show every extreme that they name: `expert_ids`: each row names 8 different experts. swap_flags[d] equals swap_flags[(d + 16) % 32]; in every draw some pairs trade and some do not.
All inputs are finite; a program needn't handle non-finite values.
Results may differ from the reference program's by a relative error of at most 0.012.
Values may be sent and summed in bfloat16 or wider, within the bound.
No kernel may reach another device: no remote copies, remote signals or barrier semaphores. Data moves between devices by JAX's collectives and lax.ppermute only.
A program may use at most 128 MiB of HBM per device.

```python
import math
import jax
import jax.numpy as jnp
from jax import lax

D = 2048
H = 768
TOP = 8
TOK_DEV = 128
EXPERTS = 32
CAP = 32
TOKENS = 16384
N_EXPERT = 32
N_DP = 4


def draw_swap_flags(key, part):
    key = jax.random.fold_in(key, 11)
    half_way = EXPERTS // 2
    pair_bits = jax.random.randint(key, (half_way,), 0, 2)
    spots = jnp.arange(half_way)
    pair_bits = jnp.where(spots == 0, 1, jnp.where(spots == half_way - 1, 1, jnp.where(spots == 1, 0, pair_bits)))
    return jnp.concatenate([pair_bits, pair_bits]).astype(jnp.int32)


def block_levels(key, extent, pieces, least, largest):
    def one(axis_at, parts):
        draws = jax.random.uniform(jax.random.fold_in(jax.random.fold_in(key, 6), axis_at), (parts,), jnp.float32, least / len(pieces), largest / len(pieces))
        return jnp.repeat(jnp.exp(draws), extent[axis_at] // parts).reshape((-1,) + (1,) * (len(extent) - axis_at - 1))

    factor_of = one(*pieces[0])
    for cut in pieces[1:]:
        factor_of = factor_of * one(*cut)
    return factor_of


def picks_of(stream_key, rows, number_of, top, lift):
    order = jax.random.permutation(jax.random.fold_in(stream_key, 1), number_of)
    pull = order
    for power in range(3):
        pull = pull * pull // number_of
    pull = pull * lift // number_of
    tickets = jax.random.randint(jax.random.fold_in(stream_key, 2), (rows, number_of), 0, 4096) + pull
    fixed_rows = jax.random.permutation(jax.random.fold_in(stream_key, 3), rows)[jnp.arange(number_of) % rows]
    tickets = jnp.where(jnp.arange(rows)[:, None] == fixed_rows[None, :], 1 << 14, tickets)
    priority = tickets * number_of + jnp.arange(number_of)
    return lax.top_k(priority.astype(jnp.int32), top)[1].astype(jnp.int32)


def normal_values(own_key, extent, scale, bound, cuts=(), held_as=jnp.bfloat16):
    array = scale * jax.random.normal(own_key, extent, jnp.float32)
    if cuts:
        array = array * block_levels(own_key, extent, cuts, -0.22, 0.18)
    return jnp.clip(array, -bound, bound).astype(held_as)


def setup_inputs(seed: int = 0) -> dict:
    keys = jax.random.split(jax.random.key(seed), 9)
    return {
        "tokens": normal_values(keys[0], (TOKENS, D), 1.0, 6.0, ((0, 128),)),
        "expert_ids": picks_of(keys[1], TOKENS, EXPERTS, TOP, 4096),
        "combine_weights": jnp.clip(jnp.exp(math.log(0.5) - 2.3025851 * jax.random.uniform(keys[2], (TOKENS, TOP), jnp.float32) ** block_levels(keys[2], (TOKENS, TOP), ((0, 128),), -0.2, 0.2)), 0.05, 0.5),
        "grad_output": normal_values(keys[3], (TOKENS, D), 1.0, 6.0, ((0, 128),)),
        "swap_flags": draw_swap_flags(jax.random.fold_in(keys[8], 71), 0),
        "w_gate": normal_values(keys[5], (EXPERTS, D, H), D ** -0.5, 0.125, ((0, 32),)),
        "w_up": normal_values(keys[6], (EXPERTS, D, H), D ** -0.5, 0.125, ((0, 32),)),
        "w_down": normal_values(keys[7], (EXPERTS, H, D), H ** -0.5, 0.21875, ((0, 32),)),
    }


def expert_forward(expert_rows, gate_w, up_w, down_w):
    gate_pre = jnp.dot(expert_rows, gate_w, preferred_element_type=jnp.float32)
    up_pre = jnp.dot(expert_rows, up_w, preferred_element_type=jnp.float32)
    sigmoid_gate = jax.nn.sigmoid(gate_pre)
    activation = (gate_pre * sigmoid_gate * up_pre).astype(jnp.bfloat16)
    expert_out = jnp.dot(activation, down_w, preferred_element_type=jnp.float32).astype(jnp.bfloat16)
    return gate_pre, up_pre, sigmoid_gate, activation, expert_out


def expert_backward(expert_rows, out_grad, gate_pre, up_pre, sigmoid_gate, activation, gate_w, up_w, down_w):
    act_grad = jnp.dot(out_grad, down_w.T, preferred_element_type=jnp.float32)
    gate_grad = (act_grad * up_pre * sigmoid_gate * (1.0 + gate_pre * (1.0 - sigmoid_gate))).astype(jnp.bfloat16)
    up_grad = (act_grad * gate_pre * sigmoid_gate).astype(jnp.bfloat16)
    row_grads = (jnp.dot(gate_grad, gate_w.T, preferred_element_type=jnp.float32)
                 + jnp.dot(up_grad, up_w.T, preferred_element_type=jnp.float32)).astype(jnp.bfloat16)
    gate_part = jnp.dot(expert_rows.T, gate_grad, preferred_element_type=jnp.float32)
    up_part = jnp.dot(expert_rows.T, up_grad, preferred_element_type=jnp.float32)
    down_part = jnp.dot(activation.T, out_grad, preferred_element_type=jnp.float32)
    return row_grads, gate_part, up_part, down_part


def replica_total(part):
    rounded = lax.optimization_barrier(part.astype(jnp.bfloat16))
    return jnp.sum(rounded.astype(jnp.float32), axis=0)


def reference(tokens, expert_ids, combine_weights, grad_output, swap_flags, w_gate, w_up, w_down):
    blocks = N_EXPERT * N_DP
    per_block = TOK_DEV * TOP
    numbers = jnp.arange(EXPERTS, dtype=jnp.int32)
    ids_blocks = expert_ids.reshape(blocks, per_block)

    def block_slots(ids_row):
        onehot = (ids_row[:, None] == numbers[None, :]).astype(jnp.int32)
        earlier = jnp.cumsum(onehot, axis=0) - onehot
        return jnp.sum(earlier * onehot, axis=1)

    slot_rank = jax.vmap(block_slots)(ids_blocks)
    retained = slot_rank < CAP
    block_index = jnp.arange(blocks, dtype=jnp.int32)[:, None]
    source = block_index // N_DP
    group = block_index % N_DP
    table_size = EXPERTS * N_DP * N_EXPERT * CAP
    position = ((ids_blocks * N_DP + group) * N_EXPERT + source) * CAP + slot_rank
    position = jnp.where(retained, position, table_size).astype(jnp.int32)
    choice_index = jnp.arange(blocks * per_block, dtype=jnp.int32).reshape(blocks, per_block)
    choice_table = jnp.full((table_size,), -1, jnp.int32)
    choice_table = choice_table.at[position.reshape(-1)].set(choice_index.reshape(-1), mode="drop")
    choice_table = choice_table.reshape(EXPERTS, N_DP, N_EXPERT * CAP)
    flat_weights = combine_weights.reshape(-1)
    grad_wide = grad_output.astype(jnp.float32)

    def per_expert(carry, inputs):
        mixed_acc, tokens_acc, weights_acc = carry
        table, gate_w, up_w, down_w = inputs
        valid = table >= 0
        safe_choice = jnp.maximum(table, 0).astype(jnp.int32)
        token_index = (safe_choice // TOP).astype(jnp.int32)
        expert_rows = jnp.where(valid[..., None], tokens[token_index], jnp.zeros((), jnp.bfloat16)).astype(jnp.bfloat16)
        row_weights = jnp.where(valid, flat_weights[safe_choice], jnp.float32(0.0))
        row_grad_out = grad_wide[token_index]
        out_grad = (row_weights[..., None] * row_grad_out).astype(jnp.bfloat16)

        def one_group(rows, grads):
            gate_pre, up_pre, sigmoid_gate, activation, expert_out = expert_forward(rows, gate_w, up_w, down_w)
            row_grads, gate_part, up_part, down_part = expert_backward(
                rows, grads, gate_pre, up_pre, sigmoid_gate, activation, gate_w, up_w, down_w)
            return expert_out, row_grads, gate_part, up_part, down_part

        expert_out, row_grads, gate_part, up_part, down_part = jax.vmap(one_group)(expert_rows, out_grad)
        out_wide = expert_out.astype(jnp.float32)
        flat_tokens = token_index.reshape(-1)
        mixed_acc = mixed_acc.at[flat_tokens].add((row_weights[..., None] * out_wide).reshape(-1, D))
        back_rows = jnp.where(valid[..., None], row_grads.astype(jnp.float32), jnp.float32(0.0))
        tokens_acc = tokens_acc.at[flat_tokens].add(back_rows.reshape(-1, D))
        products = jnp.where(valid, jnp.sum(row_grad_out * out_wide, axis=-1), jnp.float32(0.0))
        weights_acc = weights_acc.at[safe_choice.reshape(-1)].add(products.reshape(-1))
        totals = (replica_total(gate_part), replica_total(up_part), replica_total(down_part))
        return (mixed_acc, tokens_acc, weights_acc), totals

    start = (jnp.zeros((TOKENS, D), jnp.float32), jnp.zeros((TOKENS, D), jnp.float32),
             jnp.zeros((TOKENS * TOP,), jnp.float32))
    (mixed_acc, tokens_acc, weights_acc), (gate_sum, up_sum, down_sum) = lax.scan(
        per_expert, start, (choice_table, w_gate, w_up, w_down))
    holder = jnp.where(swap_flags == 1, (numbers + EXPERTS // 2) % EXPERTS, numbers).astype(jnp.int32)
    return (mixed_acc.astype(jnp.bfloat16), tokens_acc.astype(jnp.bfloat16), weights_acc.reshape(TOKENS, TOP),
            gate_sum[holder], up_sum[holder], down_sum[holder])
```

```python
import jax
import jax.numpy as jnp
from jax import lax
from jax.sharding import PartitionSpec as P


def swapped(value, axis, distance):
    mask = 2**distance
    pairs = [(source, source ^ mask) for source in range(lax.axis_size(axis))]
    return lax.ppermute(value, axis, pairs)


def expert_forward(expert_rows, gate_w, up_w, down_w):
    gate_pre = jnp.dot(expert_rows, gate_w, preferred_element_type=jnp.float32)
    up_pre = jnp.dot(expert_rows, up_w, preferred_element_type=jnp.float32)
    sigmoid_gate = jax.nn.sigmoid(gate_pre)
    activation = (gate_pre * sigmoid_gate * up_pre).astype(jnp.bfloat16)
    expert_out = jnp.dot(activation, down_w, preferred_element_type=jnp.float32).astype(
        jnp.bfloat16
    )
    return (gate_pre, up_pre, sigmoid_gate, activation, expert_out)


def expert_backward(
    expert_rows, out_grad, gate_pre, up_pre, sigmoid_gate, activation, gate_w, up_w, down_w
):
    act_grad = jnp.dot(out_grad, down_w.T, preferred_element_type=jnp.float32)
    gate_grad = (act_grad * up_pre * sigmoid_gate * (1.0 + gate_pre * (1.0 - sigmoid_gate))).astype(
        jnp.bfloat16
    )
    up_grad = (act_grad * gate_pre * sigmoid_gate).astype(jnp.bfloat16)
    row_grads = (
        jnp.dot(gate_grad, gate_w.T, preferred_element_type=jnp.float32)
        + jnp.dot(up_grad, up_w.T, preferred_element_type=jnp.float32)
    ).astype(jnp.bfloat16)
    gate_part = jnp.dot(expert_rows.T, gate_grad, preferred_element_type=jnp.float32)
    up_part = jnp.dot(expert_rows.T, up_grad, preferred_element_type=jnp.float32)
    down_part = jnp.dot(activation.T, out_grad, preferred_element_type=jnp.float32)
    return (row_grads, gate_part, up_part, down_part)


def local(tokens, expert_ids, combine_weights, grad_output, swap_flags, w_gate, w_up, w_down):
    device_count = lax.axis_size("expert")
    pair_bit = device_count.bit_length() - 2
    tok_rows, feat_width = tokens.shape
    top_k = expert_ids.shape[1]
    capacity = tok_rows * top_k // device_count
    slots_all = device_count * capacity
    device = lax.axis_index("expert")
    numbers = jnp.arange(device_count, dtype=jnp.int32)
    my_flag = jnp.sum(jnp.where(numbers == device, swap_flags, 0))
    gate_w = w_gate[0]
    up_w = w_up[0]
    down_w = w_down[0]
    target_device = expert_ids
    named = jnp.any(expert_ids[:, :, None] == numbers, axis=1)
    rows = jnp.arange(tok_rows, dtype=jnp.int32)
    before = (rows[:, None] > rows[None, :]).astype(jnp.bfloat16)
    earlier = jnp.dot(before, named.astype(jnp.bfloat16), preferred_element_type=jnp.float32)
    hits = expert_ids[:, :, None] == numbers
    slot_rank = jnp.sum(jnp.where(hits, earlier[:, None, :], 0.0), axis=2).astype(jnp.int32)
    retained = slot_rank < capacity
    target = jnp.where(
        retained, target_device * capacity + slot_rank, -1
    )
    matches = jnp.arange(slots_all, dtype=jnp.int32)[:, None, None] == target[None]
    placement = jnp.any(matches, axis=2).astype(jnp.bfloat16)
    send_tokens = jnp.dot(placement, tokens, preferred_element_type=jnp.float32).astype(
        jnp.bfloat16
    )
    kept_weights = jnp.where(retained, combine_weights, 0.0)
    slot_weight = jnp.sum(jnp.where(matches, kept_weights[None], 0.0), axis=(1, 2))
    slot_grads = jnp.dot(placement, grad_output, preferred_element_type=jnp.float32)
    send_cotangent = (slot_weight[:, None] * slot_grads).astype(jnp.bfloat16)
    expert_rows = lax.all_to_all(
        send_tokens.reshape(device_count, capacity, feat_width),
        "expert",
        split_axis=0,
        concat_axis=0,
        tiled=True,
    )
    expert_rows = expert_rows.reshape(slots_all, feat_width)
    gate_pre, up_pre, sigmoid_gate, activation, expert_out = expert_forward(
        expert_rows, gate_w, up_w, down_w
    )
    returned = lax.all_to_all(
        expert_out.reshape(device_count, capacity, feat_width),
        "expert",
        split_axis=0,
        concat_axis=0,
        tiled=True,
    )
    returned = returned.reshape(slots_all, feat_width)
    out_grad = lax.all_to_all(
        send_cotangent.reshape(device_count, capacity, feat_width),
        "expert",
        split_axis=0,
        concat_axis=0,
        tiled=True,
    )
    out_grad = out_grad.reshape(slots_all, feat_width)
    row_grads, gate_part, up_part, down_part = expert_backward(
        expert_rows, out_grad, gate_pre, up_pre, sigmoid_gate, activation, gate_w, up_w, down_w
    )
    returned_grads = lax.all_to_all(
        row_grads.reshape(device_count, capacity, feat_width),
        "expert",
        split_axis=0,
        concat_axis=0,
        tiled=True,
    )
    returned_grads = returned_grads.reshape(slots_all, feat_width)
    safe_index = jnp.maximum(target, 0)
    picked = jnp.take(returned, safe_index, axis=0).astype(jnp.float32)
    mixed = jnp.sum(kept_weights[..., None] * picked, axis=1).astype(jnp.bfloat16)
    products = jnp.sum(grad_output.astype(jnp.float32)[:, None, :] * picked, axis=2)
    grad_weights = jnp.where(retained, products, 0.0)
    picked_grads = jnp.take(returned_grads, safe_index, axis=0).astype(jnp.float32)
    grad_tokens = jnp.sum(jnp.where(retained[..., None], picked_grads, 0.0), axis=1).astype(
        jnp.bfloat16
    )
    def reduced(part, dim):
        total = lax.psum_scatter(
            part.astype(jnp.bfloat16), "dp", scatter_dimension=dim, tiled=True
        )
        partners = swapped(total, "expert", pair_bit)
        return jnp.where(my_flag == 1, partners, total).astype(jnp.float32)

    gate_sum = reduced(gate_part, 0)
    up_sum = reduced(up_part, 0)
    down_sum = reduced(down_part, 1)
    return (mixed, grad_tokens, grad_weights, gate_sum[None], up_sum[None], down_sum[None])


def solution(mesh):
    return jax.shard_map(
        local,
        mesh=mesh,
        in_specs=(
            P(("expert", "dp"), None),
            P(("expert", "dp"), None),
            P(("expert", "dp"), None),
            P(("expert", "dp"), None),
            P(),
            P("expert", None, None),
            P("expert", None, None),
            P("expert", None, None),
        ),
        out_specs=(
            P(("expert", "dp"), None),
            P(("expert", "dp"), None),
            P(("expert", "dp"), None),
            P("expert", "dp", None),
            P("expert", "dp", None),
            P("expert", None, "dp"),
        ),
        check_vma=False,
    )
```

```python
import functools

import jax
import jax.numpy as jnp
from jax import lax
from jax.experimental import pallas as pl
from jax.experimental.pallas import tpu as pltpu
from jax.sharding import PartitionSpec as P

Z, X, C = 4, 4, 2
EXPERTS = Z * X * C
SLOTS = 32
TOK = 128
BLOCK = 512
VMEM = 58 << 20
TAGS = 128
BF16, F32 = jnp.bfloat16, jnp.float32
SHORT = pl.CostEstimate(flops=1 << 20, bytes_accessed=1 << 16, transcendentals=0)


def place(z, x, c):
    return (z % Z * X + x % X) * C + c


def moved(value, dz=0, dx=0, dc=0):
    pairs = [
        (place(z, x, c), place(z + dz, x + dx, c ^ dc))
        for z in range(Z)
        for x in range(X)
        for c in range(C)
    ]
    return lax.ppermute(value, "expert", pairs)


def along(value, axis, step):
    if step % 4 == 0:
        return value
    return moved(value, dz=step) if axis == "z" else moved(value, dx=step)


def slot_matrix(tags, experts):
    turned_tags = tags.astype(F32).T
    ids, weights = turned_tags[0:8], turned_tags[8:16] + turned_tags[16:24]
    named, weight = [], []
    for i in range(4):
        hit = ids == experts[i]
        named.append(jnp.max(jnp.where(hit, 1.0, 0.0), axis=0, keepdims=True))
        weight.append(jnp.sum(jnp.where(hit, weights, 0.0), axis=0, keepdims=True))
    named = jnp.concatenate(named + named, axis=0)
    weight = jnp.concatenate(weight, axis=0)
    before = lax.broadcasted_iota(jnp.int32, (TOK, TOK), 0) < lax.broadcasted_iota(
        jnp.int32, (TOK, TOK), 1
    )
    rank = jnp.dot(
        named.astype(BF16), before.astype(F32).astype(BF16), preferred_element_type=F32
    )
    key = jnp.where(named > 0, rank, -1.0)[:4]
    slots = lax.broadcasted_iota(jnp.int32, (4, SLOTS, TOK), 1).astype(F32)
    return jnp.where(key[:, None, :] == slots, 1.0, 0.0), weight


PART = 8 * SLOTS


def slots_at(source, expert, parts):
    at = source * SLOTS + (0 if parts > 1 else PART * expert)
    return pl.ds(at, SLOTS)


def source_specs(sources, block, column):
    return [pl.BlockSpec((TOK, block), lambda i, n, r=r: (r, column(i))) for _, r in sources]


def select_kernel(weighted, parts, numbers, *refs):
    tags, sources, outs, (matrix, scale) = refs[:8], refs[8:16], refs[16:-2], refs[-2:]

    @pl.when(pl.program_id(0) == 0)
    def _():
        experts = [numbers[i].astype(F32) for i in range(4)]
        for s in range(8):
            inside, weight = slot_matrix(tags[s][...], experts)
            matrix[s] = inside.reshape(TOK, TOK).astype(BF16)
            if weighted:
                scale[s] = jnp.sum(
                    (inside * weight[:, None, :]).reshape(TOK, TOK), axis=1, keepdims=True
                )

    for s in range(8):
        rows = jnp.dot(matrix[s], sources[s][...], preferred_element_type=F32)
        if weighted:
            rows = rows * scale[s]
        rows = rows.astype(BF16)
        for i in range(4):
            outs[i % parts][slots_at(s, i, parts), :] = rows[SLOTS * i : SLOTS * (i + 1), :]


def select(numbers, sources, weighted, parts):
    width = sources[0][0].shape[1] - TAGS
    height = 4 * PART // parts
    tags = source_specs(sources, TAGS, lambda i: width // TAGS)
    return pl.pallas_call(
        functools.partial(select_kernel, weighted, parts),
        grid_spec=pltpu.PrefetchScalarGridSpec(
            num_scalar_prefetch=1,
            grid=(width // BLOCK,),
            in_specs=tags + source_specs(sources, BLOCK, lambda i: i),
            out_specs=[pl.BlockSpec((height, BLOCK), lambda i, n: (0, i))] * parts,
            scratch_shapes=[
                pltpu.VMEM((8, TOK, TOK), BF16),
                pltpu.VMEM((8, TOK, 1), F32),
            ],
        ),
        out_shape=[jax.ShapeDtypeStruct((height, width), BF16)] * parts,
        compiler_params=pltpu.CompilerParams(vmem_limit_bytes=VMEM),
        cost_estimate=SHORT,
    )(numbers, *[v for v, _ in sources], *[v for v, _ in sources])


def combine_kernel(weighted, width, parts, numbers, *refs):
    tags, rows, (own, other, matrix) = refs[:8], refs[8:-3], refs[-3:]
    step = pl.program_id(0)

    @pl.when(step == 0)
    def _():
        experts = [numbers[i].astype(F32) for i in range(4)]
        for s in range(8):
            inside, weight = slot_matrix(tags[s][...], experts)
            if weighted:
                inside = inside * weight[:, None, :]
            matrix[s] = inside.reshape(TOK, TOK).T.astype(BF16)

    for s in range(8):
        held = jnp.concatenate(
            [rows[i % parts][slots_at(s, i, parts), :] for i in range(4)], axis=0
        )
        sums = jnp.dot(matrix[s], held, preferred_element_type=F32)
        at = pl.ds(pl.multiple_of(numbers[4 + s // 2] * TOK, TOK), TOK)
        if s % 2 == 0:
            own[at, :] = sums.astype(BF16)
        elif width % BLOCK == 0:
            other[at, :] = sums.astype(BF16)
        else:
            lanes = lax.broadcasted_iota(jnp.int32, sums.shape, 1)
            apart = jnp.where((lanes >= 8) & (lanes < 16), pltpu.roll(sums, 8, 1), 0.0)
            sums = jnp.where(step == width // BLOCK, apart, sums)
            other[at, :] = sums.astype(BF16)


def combine(numbers, sources, rows, weighted):
    width = rows[0].shape[1]
    parts = len(rows)
    tags_at = (sources[0][0].shape[1] - TAGS) // TAGS
    tags = source_specs(sources, TAGS, lambda i: tags_at)
    return pl.pallas_call(
        functools.partial(combine_kernel, weighted, width, parts),
        grid_spec=pltpu.PrefetchScalarGridSpec(
            num_scalar_prefetch=1,
            grid=(pl.cdiv(width, BLOCK),),
            in_specs=tags
            + [pl.BlockSpec((4 * PART // parts, BLOCK), lambda i, n: (0, i))] * parts,
            out_specs=[pl.BlockSpec((4 * TOK, BLOCK), lambda i, n: (0, i))] * 2,
            scratch_shapes=[pltpu.VMEM((8, TOK, TOK), BF16)],
        ),
        compiler_params=pltpu.CompilerParams(vmem_limit_bytes=VMEM),
        out_shape=[jax.ShapeDtypeStruct((4 * TOK, width), BF16)] * 2,
        cost_estimate=SHORT,
    )(numbers, *[v for v, _ in sources], *rows)


def forward_kernel(rows, gate_w, up_w, gate_pre, up_pre, activation):
    gate = dot(rows[...], gate_w[...], ((1,), (0,)))
    up = dot(rows[...], up_w[...], ((1,), (0,)))
    gate_pre[...] = gate
    up_pre[...] = up
    activation[...] = (gate * jax.nn.sigmoid(gate) * up).astype(BF16)


def forward(rows, gate_w, up_w):
    count, width = rows.shape
    hidden = gate_w.shape[1]
    weights = pl.BlockSpec((width, hidden), lambda i: (0, 0))
    block = pl.BlockSpec((PART, hidden), lambda i: (i, 0))
    shapes = [jax.ShapeDtypeStruct((count, hidden), t) for t in (F32, F32, BF16)]
    return pl.pallas_call(
        forward_kernel,
        grid=(count // PART,),
        in_specs=[pl.BlockSpec((PART, width), lambda i: (i, 0)), weights, weights],
        out_specs=[block] * 3,
        out_shape=shapes,
        compiler_params=pltpu.CompilerParams(vmem_limit_bytes=VMEM),
        cost_estimate=SHORT,
    )(rows, gate_w, up_w)


def out_kernel(activation, down_w, out):
    out[...] = dot(activation[...], down_w[...], ((1,), (0,))).astype(BF16)


def expert_output(activation, down_w):
    count, hidden = activation.shape
    width = down_w.shape[1]
    return pl.pallas_call(
        out_kernel,
        grid=(count // PART,),
        in_specs=[
            pl.BlockSpec((PART, hidden), lambda i: (i, 0)),
            pl.BlockSpec((hidden, width), lambda i: (0, 0)),
        ],
        out_specs=pl.BlockSpec((PART, width), lambda i: (i, 0)),
        out_shape=jax.ShapeDtypeStruct((count, width), BF16),
        compiler_params=pltpu.CompilerParams(vmem_limit_bytes=VMEM),
        cost_estimate=SHORT,
    )(activation, down_w)


def backward_kernel(g0, g1, g2, g3, down_w, gate_pre, up_pre, activation, *refs):
    gate_grad, up_grad, slots, down_part = refs
    grads, run = (g0, g1, g2, g3), C * SLOTS
    act = activation[...]
    down = None
    act_grads = []
    for j in range(4):
        act_grads.append(dot(grads[j][...], down_w[...], ((1,), (1,))))
        turned_act = jnp.concatenate(
            [act[(4 * k + j) * run : (4 * k + j + 1) * run] for k in range(4)], axis=0
        )
        term = dot(turned_act, grads[j][...], ((0,), (0,)))
        down = term if down is None else down + term
    down_part[...] = down.astype(BF16)
    for k in range(4):
        at = slice(k * PART, (k + 1) * PART)
        act_grad = jnp.concatenate(
            [act_grads[j][k * run : (k + 1) * run] for j in range(4)], axis=0
        )
        gate, up = gate_pre[at, :], up_pre[at, :]
        sigmoid = jax.nn.sigmoid(gate)
        gate_grad[at, :] = (act_grad * up * sigmoid * (1.0 + gate * (1.0 - sigmoid))).astype(BF16)
        up_grad[at, :] = (act_grad * gate * sigmoid).astype(BF16)
        term = jnp.sum(act[at].astype(F32) * act_grad, axis=1, keepdims=True)

        @pl.when(pl.program_id(0) == 0)
        def _(at=at, term=term):
            slots[at, :] = term

        @pl.when(pl.program_id(0) > 0)
        def _(at=at, term=term):
            slots[at, :] += term


def backward(grads, down_w, gate_pre, up_pre, activation):
    hidden, width = down_w.shape
    count, step = activation.shape[0], 256
    column = pl.BlockSpec((count, step), lambda i: (0, i))
    weights = pl.BlockSpec((step, width), lambda i: (i, 0))
    return pl.pallas_call(
        backward_kernel,
        grid=(hidden // step,),
        in_specs=[pl.BlockSpec((PART, width), lambda i: (0, 0))] * 4 + [weights] + [column] * 3,
        out_specs=[column, column, pl.BlockSpec((count, 1), lambda i: (0, 0)), weights],
        out_shape=[
            jax.ShapeDtypeStruct((count, hidden), BF16),
            jax.ShapeDtypeStruct((count, hidden), BF16),
            jax.ShapeDtypeStruct((count, 1), F32),
            jax.ShapeDtypeStruct((hidden, width), BF16),
        ],
        compiler_params=pltpu.CompilerParams(vmem_limit_bytes=VMEM),
        cost_estimate=SHORT,
    )(*grads, down_w, gate_pre, up_pre, activation)


def part_kernel(rows, grad, out):
    out[...] = dot(rows[...], grad[...], ((0,), (0,))).astype(BF16)


def weight_part(rows, grad):
    count, width = rows.shape
    hidden = grad.shape[1]
    return pl.pallas_call(
        part_kernel,
        grid=(width // BLOCK,),
        in_specs=[
            pl.BlockSpec((count, BLOCK), lambda i: (0, i)),
            pl.BlockSpec((count, hidden), lambda i: (0, 0)),
        ],
        out_specs=pl.BlockSpec((BLOCK, hidden), lambda i: (i, 0)),
        out_shape=jax.ShapeDtypeStruct((width, hidden), BF16),
        compiler_params=pltpu.CompilerParams(vmem_limit_bytes=VMEM),
        cost_estimate=SHORT,
    )(rows, grad)


def row_kernel(steps, gate_grad, up_grad, gate_w, up_w, high, low, *outs):
    step = pl.program_id(0)

    def put(rows):
        for k in range(4):
            for j in range(4):
                at = (k * 4 + j) * C * SLOTS
                outs[j][k * C * SLOTS : (k + 1) * C * SLOTS, :] = rows(j, at, at + C * SLOTS)

    @pl.when(step < steps)
    def _():
        wide = dot(gate_grad[...], gate_w[...], ((1,), (1,)))
        wide = (wide + dot(up_grad[...], up_w[...], ((1,), (1,)))).astype(BF16)
        put(lambda j, a, b: wide[a:b])

    @pl.when(step == steps)
    def _():
        lanes = lax.broadcasted_iota(jnp.int32, (C * SLOTS, BLOCK), 1)

        def rows(j, a, b):
            upper = jnp.where(lanes == j, high[a:b].astype(F32), 0.0)
            return jnp.where(lanes == 4 + j, low[a:b].astype(F32), upper).astype(BF16)

        put(rows)


def row_gradients(gate_grad, up_grad, gate_w, up_w, high, low):
    width, hidden = gate_w.shape
    steps = width // BLOCK
    whole = pl.BlockSpec(gate_grad.shape, lambda i: (0, 0))
    weights = pl.BlockSpec((BLOCK, hidden), lambda i: (jnp.minimum(i, steps - 1), 0))
    column = pl.BlockSpec(high.shape, lambda i: (0, 0))
    return pl.pallas_call(
        functools.partial(row_kernel, steps),
        grid=(steps + 1,),
        in_specs=[whole, whole, weights, weights, column, column],
        out_specs=[pl.BlockSpec((8 * SLOTS, BLOCK), lambda i: (0, i))] * 4,
        out_shape=[jax.ShapeDtypeStruct((8 * SLOTS, width + TAGS), BF16)] * 4,
        compiler_params=pltpu.CompilerParams(vmem_limit_bytes=VMEM),
        cost_estimate=SHORT,
    )(gate_grad, up_grad, gate_w, up_w, high, low)


def dot(a, b, contract):
    return lax.dot_general(a, b, (contract, ((), ())), preferred_element_type=F32)


def after(value, *earlier):
    return lax.optimization_barrier((value, earlier))[0]


def halves(value):
    high = value.astype(BF16)
    return high, (value - high.astype(F32)).astype(BF16)


def core_sum(parts):
    own, other = parts
    return (own.astype(F32) + moved(other, dc=1).astype(F32)).astype(BF16)


def after(value, *earlier):
    return lax.optimization_barrier((value, earlier))[0]


def halves(value):
    high = value.astype(BF16)
    return high, (value - high.astype(F32)).astype(BF16)


def core_sum(parts):
    own, other = parts
    return (own.astype(F32) + moved(other, dc=1).astype(F32)).astype(BF16)


def home(sums, axis):
    return [along(v, axis, -i).astype(F32) for i, v in enumerate(sums)]


def local(tokens, expert_ids, combine_weights, grad_output, swap_flags, w_gate, w_up, w_down):
    width = tokens.shape[1]
    me = lax.axis_index("expert")
    z, x, c = me // (X * C), me // C % X, me % C
    gate_w, up_w, down_w = w_gate[0], w_up[0], w_down[0]
    high, low = halves(combine_weights)
    tags = jnp.concatenate(
        [expert_ids.astype(BF16), high, low, jnp.zeros((TOK, TAGS - 24), BF16)], axis=1
    )

    along_x = [[place(i, j, k) for j in range(X)] for i in range(Z) for k in range(C)]
    along_z = [[place(i, j, k) for i in range(Z)] for j in range(X) for k in range(C)]

    def exchanged(v, groups=along_x):
        parts = v.reshape(4, -1, v.shape[1])
        parts = lax.all_to_all(parts, "expert", 0, 0, axis_index_groups=groups, tiled=True)
        return parts.reshape(v.shape)

    tagged = jnp.concatenate([tokens, tags], axis=1)
    legs = [along(tagged, "z", j) for j in range(4)]
    token_parts = [(v, 0) for part in legs for v in (part, moved(part, dc=1))]
    tagged = jnp.concatenate([grad_output, tags], axis=1)
    gathered = exchanged(jnp.concatenate([tagged] * X, axis=0))
    arrived = moved(gathered, dc=1)
    cotangent_parts = [(v, i) for i in range(X) for v in (gathered, arrived)]
    by_x = jnp.stack(
        [place(z, i, c) for i in range(X)] + [(z - j) % Z for j in range(4)]
    ).astype(jnp.int32)
    by_z = jnp.stack(
        [place(z + j, x, c) for j in range(4)] + [(x - i) % X for i in range(X)]
    ).astype(jnp.int32)

    rows = exchanged(select(by_x, token_parts, False, 1)[0])
    sent = select(by_z, cotangent_parts, True, 4)
    grads = [along(v, "z", j) for j, v in enumerate(sent)]

    gate_pre, up_pre, activation = forward(rows, gate_w, up_w)
    expert_out = expert_output(activation, down_w)
    back = exchanged(expert_out)
    gate_grad, up_grad, weight_slots, down_part = backward(
        grads, down_w, gate_pre, up_pre, after(activation, expert_out)
    )
    gate_part = weight_part(rows, gate_grad)
    gate_grad, up_grad, weight_slots = after((gate_grad, up_grad, weight_slots), gate_part)
    back_grads = row_gradients(gate_grad, up_grad, gate_w, up_w, *halves(weight_slots))
    back_grads = [along(v, "z", -j) for j, v in enumerate(back_grads)]
    numbers = jnp.arange(EXPERTS, dtype=jnp.int32)
    my_flag = jnp.sum(jnp.where(numbers == me, swap_flags, 0))

    def with_partners(mine):
        return mine, moved(mine, dz=Z // 2)

    def traded(pair):
        return jnp.where(my_flag == 1, pair[1], pair[0]).astype(F32)[None]

    down_pair = with_partners(lax.psum_scatter(down_part, "dp", scatter_dimension=1, tiled=True))
    up_part = weight_part(rows, after(up_grad, back, back_grads, down_pair))
    gate_pair = with_partners(lax.psum_scatter(gate_part, "dp", scatter_dimension=0, tiled=True))
    up_pair = with_partners(lax.psum_scatter(up_part, "dp", scatter_dimension=0, tiled=True))

    back = after(back, up_part, back_grads, down_pair)
    token_sums = core_sum(combine(by_x, token_parts, [back], True))
    cotangent_sums = core_sum(combine(after(by_z, token_sums), cotangent_parts, back_grads, False))
    arrived = exchanged(token_sums, along_z).reshape(Z, TOK, width)
    mixed = jnp.sum(arrived.astype(F32), axis=0).astype(BF16)
    cotangent_sums = after(cotangent_sums, token_sums)
    parts = [
        along(cotangent_sums[TOK * k : TOK * (k + 1)], "x", -k).astype(F32) for k in range(4)
    ]
    grad_tokens = sum(v[:, :width] for v in parts).astype(BF16)
    down_sum = traded(down_pair)
    gate_sum, up_sum = [traded(after(v, token_sums, cotangent_sums)) for v in (gate_pair, up_pair)]
    of_expert = jnp.concatenate([v[:, width : width + 16] for v in parts], axis=1)
    expert_at = jnp.stack(
        [place(z + j, x + k, c ^ b) for k in range(4) for b in range(C) for _ in range(2) for j in range(4)]
    )
    grad_weights = (
        jnp.sum(
            jnp.where(expert_ids[:, :, None] == expert_at, of_expert[:, None, :], 0.0), axis=2
        )
        / combine_weights
    )

    return (mixed, grad_tokens, grad_weights, gate_sum, up_sum, down_sum)


def solution(mesh):
    return jax.shard_map(
        local,
        mesh=mesh,
        in_specs=(
            P(("expert", "dp"), None),
            P(("expert", "dp"), None),
            P(("expert", "dp"), None),
            P(("expert", "dp"), None),
            P(),
            P("expert", None, None),
            P("expert", None, None),
            P("expert", None, None),
        ),
        out_specs=(
            P(("expert", "dp"), None),
            P(("expert", "dp"), None),
            P(("expert", "dp"), None),
            P("expert", "dp", None),
            P("expert", "dp", None),
            P("expert", None, "dp"),
        ),
        check_vma=False,
    )
```

```python
import functools

import jax
import jax.numpy as jnp
from jax import lax
from jax.experimental import pallas as pl
from jax.experimental.pallas import tpu as pltpu
from jax.sharding import PartitionSpec as P

Z, X, C = 4, 4, 2
EXPERTS = Z * X * C
SLOTS = 32
TOK = 128
BLOCK = 512
VMEM = 58 << 20
TAGS = 128
BF16, F32 = jnp.bfloat16, jnp.float32
SHORT = pl.CostEstimate(flops=1 << 20, bytes_accessed=1 << 16, transcendentals=0)


def place(z, x, c):
    return (z % Z * X + x % X) * C + c


def moved(value, dz=0, dx=0, dc=0):
    pairs = [
        (place(z, x, c), place(z + dz, x + dx, c ^ dc))
        for z in range(Z)
        for x in range(X)
        for c in range(C)
    ]
    return lax.ppermute(value, "expert", pairs)


def along(value, axis, step):
    if step % 4 == 0:
        return value
    return moved(value, dz=step) if axis == "z" else moved(value, dx=step)


def slot_matrix(tags, experts):
    turned_tags = tags.astype(F32).T
    ids, weights = turned_tags[0:8], turned_tags[8:16] + turned_tags[16:24]
    named, weight = [], []
    for i in range(4):
        hit = ids == experts[i]
        named.append(jnp.max(jnp.where(hit, 1.0, 0.0), axis=0, keepdims=True))
        weight.append(jnp.sum(jnp.where(hit, weights, 0.0), axis=0, keepdims=True))
    named = jnp.concatenate(named + named, axis=0)
    weight = jnp.concatenate(weight, axis=0)
    before = lax.broadcasted_iota(jnp.int32, (TOK, TOK), 0) < lax.broadcasted_iota(
        jnp.int32, (TOK, TOK), 1
    )
    rank = jnp.dot(
        named.astype(BF16), before.astype(F32).astype(BF16), preferred_element_type=F32
    )
    key = jnp.where(named > 0, rank, -1.0)[:4]
    slots = lax.broadcasted_iota(jnp.int32, (4, SLOTS, TOK), 1).astype(F32)
    return jnp.where(key[:, None, :] == slots, 1.0, 0.0), weight


PART = 8 * SLOTS


def slots_at(source, expert, parts):
    at = source * SLOTS + (0 if parts > 1 else PART * expert)
    return pl.ds(at, SLOTS)


def source_specs(sources, block, column):
    return [pl.BlockSpec((TOK, block), lambda i, n, r=r: (r, column(i))) for _, r in sources]


def select_kernel(weighted, parts, numbers, *refs):
    tags, sources, outs, (matrix, scale) = refs[:8], refs[8:16], refs[16:-2], refs[-2:]

    @pl.when(pl.program_id(0) == 0)
    def _():
        experts = [numbers[i].astype(F32) for i in range(4)]
        for s in range(8):
            inside, weight = slot_matrix(tags[s][...], experts)
            matrix[s] = inside.reshape(TOK, TOK).astype(BF16)
            if weighted:
                scale[s] = jnp.sum(
                    (inside * weight[:, None, :]).reshape(TOK, TOK), axis=1, keepdims=True
                )

    for s in range(8):
        rows = jnp.dot(matrix[s], sources[s][...], preferred_element_type=F32)
        if weighted:
            rows = rows * scale[s]
        rows = rows.astype(BF16)
        for i in range(4):
            outs[i % parts][slots_at(s, i, parts), :] = rows[SLOTS * i : SLOTS * (i + 1), :]


def select(numbers, sources, weighted, parts):
    width = sources[0][0].shape[1] - TAGS
    height = 4 * PART // parts
    tags = source_specs(sources, TAGS, lambda i: width // TAGS)
    return pl.pallas_call(
        functools.partial(select_kernel, weighted, parts),
        grid_spec=pltpu.PrefetchScalarGridSpec(
            num_scalar_prefetch=1,
            grid=(width // BLOCK,),
            in_specs=tags + source_specs(sources, BLOCK, lambda i: i),
            out_specs=[pl.BlockSpec((height, BLOCK), lambda i, n: (0, i))] * parts,
            scratch_shapes=[
                pltpu.VMEM((8, TOK, TOK), BF16),
                pltpu.VMEM((8, TOK, 1), F32),
            ],
        ),
        out_shape=[jax.ShapeDtypeStruct((height, width), BF16)] * parts,
        compiler_params=pltpu.CompilerParams(vmem_limit_bytes=VMEM),
        cost_estimate=SHORT,
    )(numbers, *[v for v, _ in sources], *[v for v, _ in sources])


def combine_kernel(weighted, width, parts, numbers, *refs):
    tags, rows, (own, other, matrix) = refs[:8], refs[8:-3], refs[-3:]
    step = pl.program_id(0)

    @pl.when(step == 0)
    def _():
        experts = [numbers[i].astype(F32) for i in range(4)]
        for s in range(8):
            inside, weight = slot_matrix(tags[s][...], experts)
            if weighted:
                inside = inside * weight[:, None, :]
            matrix[s] = inside.reshape(TOK, TOK).T.astype(BF16)

    for s in range(8):
        held = jnp.concatenate(
            [rows[i % parts][slots_at(s, i, parts), :] for i in range(4)], axis=0
        )
        sums = jnp.dot(matrix[s], held, preferred_element_type=F32)
        at = pl.ds(pl.multiple_of(numbers[4 + s // 2] * TOK, TOK), TOK)
        if s % 2 == 0:
            own[at, :] = sums.astype(BF16)
        elif width % BLOCK == 0:
            other[at, :] = sums.astype(BF16)
        else:
            lanes = lax.broadcasted_iota(jnp.int32, sums.shape, 1)
            apart = jnp.where((lanes >= 8) & (lanes < 16), pltpu.roll(sums, 8, 1), 0.0)
            sums = jnp.where(step == width // BLOCK, apart, sums)
            other[at, :] = sums.astype(BF16)


def combine(numbers, sources, rows, weighted):
    width = rows[0].shape[1]
    parts = len(rows)
    tags_at = (sources[0][0].shape[1] - TAGS) // TAGS
    tags = source_specs(sources, TAGS, lambda i: tags_at)
    return pl.pallas_call(
        functools.partial(combine_kernel, weighted, width, parts),
        grid_spec=pltpu.PrefetchScalarGridSpec(
            num_scalar_prefetch=1,
            grid=(pl.cdiv(width, BLOCK),),
            in_specs=tags
            + [pl.BlockSpec((4 * PART // parts, BLOCK), lambda i, n: (0, i))] * parts,
            out_specs=[pl.BlockSpec((4 * TOK, BLOCK), lambda i, n: (0, i))] * 2,
            scratch_shapes=[pltpu.VMEM((8, TOK, TOK), BF16)],
        ),
        compiler_params=pltpu.CompilerParams(vmem_limit_bytes=VMEM),
        out_shape=[jax.ShapeDtypeStruct((4 * TOK, width), BF16)] * 2,
        cost_estimate=SHORT,
    )(numbers, *[v for v, _ in sources], *rows)


def forward_kernel(rows, gate_w, up_w, gate_pre, up_pre, activation):
    gate = dot(rows[...], gate_w[...], ((1,), (0,)))
    up = dot(rows[...], up_w[...], ((1,), (0,)))
    gate_pre[...] = gate
    up_pre[...] = up
    activation[...] = (gate * jax.nn.sigmoid(gate) * up).astype(BF16)


def forward(rows, gate_w, up_w):
    count, width = rows.shape
    hidden = gate_w.shape[1]
    weights = pl.BlockSpec((width, hidden), lambda i: (0, 0))
    block = pl.BlockSpec((PART, hidden), lambda i: (i, 0))
    shapes = [jax.ShapeDtypeStruct((count, hidden), t) for t in (F32, F32, BF16)]
    return pl.pallas_call(
        forward_kernel,
        grid=(count // PART,),
        in_specs=[pl.BlockSpec((PART, width), lambda i: (i, 0)), weights, weights],
        out_specs=[block] * 3,
        out_shape=shapes,
        compiler_params=pltpu.CompilerParams(vmem_limit_bytes=VMEM),
        cost_estimate=SHORT,
    )(rows, gate_w, up_w)


def out_kernel(activation, down_w, out):
    out[...] = dot(activation[...], down_w[...], ((1,), (0,))).astype(BF16)


def expert_output(activation, down_w):
    count, hidden = activation.shape
    width = down_w.shape[1]
    return pl.pallas_call(
        out_kernel,
        grid=(count // PART,),
        in_specs=[
            pl.BlockSpec((PART, hidden), lambda i: (i, 0)),
            pl.BlockSpec((hidden, width), lambda i: (0, 0)),
        ],
        out_specs=pl.BlockSpec((PART, width), lambda i: (i, 0)),
        out_shape=jax.ShapeDtypeStruct((count, width), BF16),
        compiler_params=pltpu.CompilerParams(vmem_limit_bytes=VMEM),
        cost_estimate=SHORT,
    )(activation, down_w)


def backward_kernel(g0, g1, g2, g3, down_w, gate_pre, up_pre, activation, *refs):
    gate_grad, up_grad, slots, down_part = refs
    grads, run = (g0, g1, g2, g3), C * SLOTS
    act = activation[...]
    down = None
    act_grads = []
    for j in range(4):
        act_grads.append(dot(grads[j][...], down_w[...], ((1,), (1,))))
        turned_act = jnp.concatenate(
            [act[(4 * k + j) * run : (4 * k + j + 1) * run] for k in range(4)], axis=0
        )
        term = dot(turned_act, grads[j][...], ((0,), (0,)))
        down = term if down is None else down + term
    down_part[...] = down.astype(BF16)
    for k in range(4):
        at = slice(k * PART, (k + 1) * PART)
        act_grad = jnp.concatenate(
            [act_grads[j][k * run : (k + 1) * run] for j in range(4)], axis=0
        )
        gate, up = gate_pre[at, :], up_pre[at, :]
        sigmoid = jax.nn.sigmoid(gate)
        gate_grad[at, :] = (act_grad * up * sigmoid * (1.0 + gate * (1.0 - sigmoid))).astype(BF16)
        up_grad[at, :] = (act_grad * gate * sigmoid).astype(BF16)
        term = jnp.sum(act[at].astype(F32) * act_grad, axis=1, keepdims=True)

        @pl.when(pl.program_id(0) == 0)
        def _(at=at, term=term):
            slots[at, :] = term

        @pl.when(pl.program_id(0) > 0)
        def _(at=at, term=term):
            slots[at, :] += term


def backward(grads, down_w, gate_pre, up_pre, activation):
    hidden, width = down_w.shape
    count, step = activation.shape[0], 256
    column = pl.BlockSpec((count, step), lambda i: (0, i))
    weights = pl.BlockSpec((step, width), lambda i: (i, 0))
    return pl.pallas_call(
        backward_kernel,
        grid=(hidden // step,),
        in_specs=[pl.BlockSpec((PART, width), lambda i: (0, 0))] * 4 + [weights] + [column] * 3,
        out_specs=[column, column, pl.BlockSpec((count, 1), lambda i: (0, 0)), weights],
        out_shape=[
            jax.ShapeDtypeStruct((count, hidden), BF16),
            jax.ShapeDtypeStruct((count, hidden), BF16),
            jax.ShapeDtypeStruct((count, 1), F32),
            jax.ShapeDtypeStruct((hidden, width), BF16),
        ],
        compiler_params=pltpu.CompilerParams(vmem_limit_bytes=VMEM),
        cost_estimate=SHORT,
    )(*grads, down_w, gate_pre, up_pre, activation)


def part_kernel(rows, grad, out):
    out[...] = dot(rows[...], grad[...], ((0,), (0,))).astype(BF16)


def weight_part(rows, grad):
    count, width = rows.shape
    hidden = grad.shape[1]
    return pl.pallas_call(
        part_kernel,
        grid=(width // BLOCK,),
        in_specs=[
            pl.BlockSpec((count, BLOCK), lambda i: (0, i)),
            pl.BlockSpec((count, hidden), lambda i: (0, 0)),
        ],
        out_specs=pl.BlockSpec((BLOCK, hidden), lambda i: (i, 0)),
        out_shape=jax.ShapeDtypeStruct((width, hidden), BF16),
        compiler_params=pltpu.CompilerParams(vmem_limit_bytes=VMEM),
        cost_estimate=SHORT,
    )(rows, grad)


def row_kernel(steps, gate_grad, up_grad, gate_w, up_w, high, low, *outs):
    step = pl.program_id(0)

    def put(rows):
        for k in range(4):
            for j in range(4):
                at = (k * 4 + j) * C * SLOTS
                outs[j][k * C * SLOTS : (k + 1) * C * SLOTS, :] = rows(j, at, at + C * SLOTS)

    @pl.when(step < steps)
    def _():
        wide = dot(gate_grad[...], gate_w[...], ((1,), (1,)))
        wide = (wide + dot(up_grad[...], up_w[...], ((1,), (1,)))).astype(BF16)
        put(lambda j, a, b: wide[a:b])

    @pl.when(step == steps)
    def _():
        lanes = lax.broadcasted_iota(jnp.int32, (C * SLOTS, BLOCK), 1)

        def rows(j, a, b):
            upper = jnp.where(lanes == j, high[a:b].astype(F32), 0.0)
            return jnp.where(lanes == 4 + j, low[a:b].astype(F32), upper).astype(BF16)

        put(rows)


def row_gradients(gate_grad, up_grad, gate_w, up_w, high, low):
    width, hidden = gate_w.shape
    steps = width // BLOCK
    whole = pl.BlockSpec(gate_grad.shape, lambda i: (0, 0))
    weights = pl.BlockSpec((BLOCK, hidden), lambda i: (jnp.minimum(i, steps - 1), 0))
    column = pl.BlockSpec(high.shape, lambda i: (0, 0))
    return pl.pallas_call(
        functools.partial(row_kernel, steps),
        grid=(steps + 1,),
        in_specs=[whole, whole, weights, weights, column, column],
        out_specs=[pl.BlockSpec((8 * SLOTS, BLOCK), lambda i: (0, i))] * 4,
        out_shape=[jax.ShapeDtypeStruct((8 * SLOTS, width + TAGS), BF16)] * 4,
        compiler_params=pltpu.CompilerParams(vmem_limit_bytes=VMEM),
        cost_estimate=SHORT,
    )(gate_grad, up_grad, gate_w, up_w, high, low)


def dot(a, b, contract):
    return lax.dot_general(a, b, (contract, ((), ())), preferred_element_type=F32)


def after(value, *earlier):
    return lax.optimization_barrier((value, earlier))[0]


def halves(value):
    high = value.astype(BF16)
    return high, (value - high.astype(F32)).astype(BF16)


def core_sum(parts):
    own, other = parts
    return (own.astype(F32) + moved(other, dc=1).astype(F32)).astype(BF16)


def after(value, *earlier):
    return lax.optimization_barrier((value, earlier))[0]


def halves(value):
    high = value.astype(BF16)
    return high, (value - high.astype(F32)).astype(BF16)


def core_sum(parts):
    own, other = parts
    return (own.astype(F32) + moved(other, dc=1).astype(F32)).astype(BF16)


def home(sums, axis):
    return [along(v, axis, -i).astype(F32) for i, v in enumerate(sums)]


def local(tokens, expert_ids, combine_weights, grad_output, swap_flags, w_gate, w_up, w_down):
    width = tokens.shape[1]
    me = lax.axis_index("expert")
    z, x, c = me // (X * C), me // C % X, me % C
    gate_w, up_w, down_w = w_gate[0], w_up[0], w_down[0]
    high, low = halves(combine_weights)
    tags = jnp.concatenate(
        [expert_ids.astype(BF16), high, low, jnp.zeros((TOK, TAGS - 24), BF16)], axis=1
    )

    along_x = [[place(i, j, k) for j in range(X)] for i in range(Z) for k in range(C)]
    along_z = [[place(i, j, k) for i in range(Z)] for j in range(X) for k in range(C)]

    def exchanged(v, groups=along_x):
        parts = v.reshape(4, -1, v.shape[1])
        parts = lax.all_to_all(parts, "expert", 0, 0, axis_index_groups=groups, tiled=True)
        return parts.reshape(v.shape)

    tagged = jnp.concatenate([tokens, tags], axis=1)
    legs = [along(tagged, "z", j) for j in range(4)]
    token_parts = [(v, 0) for part in legs for v in (part, moved(part, dc=1))]
    tagged = jnp.concatenate([grad_output, tags], axis=1)
    gathered = exchanged(jnp.concatenate([tagged] * X, axis=0))
    arrived = moved(gathered, dc=1)
    cotangent_parts = [(v, i) for i in range(X) for v in (gathered, arrived)]
    by_x = jnp.stack(
        [place(z, i, c) for i in range(X)] + [(z - j) % Z for j in range(4)]
    ).astype(jnp.int32)
    by_z = jnp.stack(
        [place(z + j, x, c) for j in range(4)] + [(x - i) % X for i in range(X)]
    ).astype(jnp.int32)

    rows = exchanged(select(by_x, token_parts, False, 1)[0])
    sent = select(by_z, cotangent_parts, True, 4)
    grads = [along(v, "z", j) for j, v in enumerate(sent)]

    gate_pre, up_pre, activation = forward(rows, gate_w, up_w)
    expert_out = expert_output(activation, down_w)
    back = exchanged(expert_out)
    gate_grad, up_grad, weight_slots, down_part = backward(
        grads, down_w, gate_pre, up_pre, after(activation, expert_out)
    )
    gate_part = weight_part(rows, gate_grad)
    gate_grad, up_grad, weight_slots = after((gate_grad, up_grad, weight_slots), gate_part)
    back_grads = row_gradients(gate_grad, up_grad, gate_w, up_w, *halves(weight_slots))
    back_grads = [along(v, "z", -j) for j, v in enumerate(back_grads)]
    numbers = jnp.arange(EXPERTS, dtype=jnp.int32)
    my_flag = jnp.sum(jnp.where(numbers == me, swap_flags, 0))

    def with_partners(mine):
        return mine, moved(mine, dz=Z // 2)

    def traded(pair):
        return jnp.where(my_flag == 1, pair[1], pair[0]).astype(F32)[None]

    down_pair = with_partners(lax.psum_scatter(down_part, "dp", scatter_dimension=1, tiled=True))
    up_part = weight_part(rows, after(up_grad, back_grads))
    gate_pair = with_partners(lax.psum_scatter(gate_part, "dp", scatter_dimension=0, tiled=True))
    up_pair = with_partners(lax.psum_scatter(up_part, "dp", scatter_dimension=0, tiled=True))

    back = after(back, up_part, back_grads)
    token_sums = combine(by_x, token_parts, [back], True)
    token_sums = core_sum(after(token_sums, down_pair))
    cotangent_sums = core_sum(combine(after(by_z, token_sums), cotangent_parts, back_grads, False))
    arrived = exchanged(token_sums, along_z).reshape(Z, TOK, width)
    mixed = jnp.sum(arrived.astype(F32), axis=0).astype(BF16)
    cotangent_sums = after(cotangent_sums, token_sums)
    parts = [
        along(cotangent_sums[TOK * k : TOK * (k + 1)], "x", -k).astype(F32) for k in range(4)
    ]
    grad_tokens = sum(v[:, :width] for v in parts).astype(BF16)
    down_sum = traded(down_pair)
    gate_sum, up_sum = [traded(after(v, token_sums, cotangent_sums)) for v in (gate_pair, up_pair)]
    of_expert = jnp.concatenate([v[:, width : width + 16] for v in parts], axis=1)
    expert_at = jnp.stack(
        [place(z + j, x + k, c ^ b) for k in range(4) for b in range(C) for _ in range(2) for j in range(4)]
    )
    grad_weights = (
        jnp.sum(
            jnp.where(expert_ids[:, :, None] == expert_at, of_expert[:, None, :], 0.0), axis=2
        )
        / combine_weights
    )

    return (mixed, grad_tokens, grad_weights, gate_sum, up_sum, down_sum)


def solution(mesh):
    return jax.shard_map(
        local,
        mesh=mesh,
        in_specs=(
            P(("expert", "dp"), None),
            P(("expert", "dp"), None),
            P(("expert", "dp"), None),
            P(("expert", "dp"), None),
            P(),
            P("expert", None, None),
            P("expert", None, None),
            P("expert", None, None),
        ),
        out_specs=(
            P(("expert", "dp"), None),
            P(("expert", "dp"), None),
            P(("expert", "dp"), None),
            P("expert", "dp", None),
            P("expert", "dp", None),
            P("expert", None, "dp"),
        ),
        check_vma=False,
    )
```

```python
import functools

import jax
import jax.numpy as jnp
from jax import lax
from jax.experimental import pallas as pl
from jax.experimental.pallas import tpu as pltpu
from jax.sharding import PartitionSpec as P

Z, X, C = 4, 4, 2
EXPERTS = Z * X * C
SLOTS = 32
TOK = 128
BLOCK = 512
VMEM = 58 << 20
TAGS = 128
BF16, F32 = jnp.bfloat16, jnp.float32
SHORT = pl.CostEstimate(flops=1 << 20, bytes_accessed=1 << 16, transcendentals=0)


def place(z, x, c):
    return (z % Z * X + x % X) * C + c


def moved(value, dz=0, dx=0, dc=0):
    pairs = [
        (place(z, x, c), place(z + dz, x + dx, c ^ dc))
        for z in range(Z)
        for x in range(X)
        for c in range(C)
    ]
    return lax.ppermute(value, "expert", pairs)


def along(value, axis, step):
    if step % 4 == 0:
        return value
    return moved(value, dz=step) if axis == "z" else moved(value, dx=step)


def slot_matrix(tags, experts):
    turned_tags = tags.astype(F32).T
    ids, weights = turned_tags[0:8], turned_tags[8:16] + turned_tags[16:24]
    named, weight = [], []
    for i in range(4):
        hit = ids == experts[i]
        named.append(jnp.max(jnp.where(hit, 1.0, 0.0), axis=0, keepdims=True))
        weight.append(jnp.sum(jnp.where(hit, weights, 0.0), axis=0, keepdims=True))
    named = jnp.concatenate(named + named, axis=0)
    weight = jnp.concatenate(weight, axis=0)
    before = lax.broadcasted_iota(jnp.int32, (TOK, TOK), 0) < lax.broadcasted_iota(
        jnp.int32, (TOK, TOK), 1
    )
    rank = jnp.dot(
        named.astype(BF16), before.astype(F32).astype(BF16), preferred_element_type=F32
    )
    key = jnp.where(named > 0, rank, -1.0)[:4]
    slots = lax.broadcasted_iota(jnp.int32, (4, SLOTS, TOK), 1).astype(F32)
    return jnp.where(key[:, None, :] == slots, 1.0, 0.0), weight


PART = 8 * SLOTS


def slots_at(source, expert, parts):
    at = source * SLOTS + (0 if parts > 1 else PART * expert)
    return pl.ds(at, SLOTS)


def source_specs(sources, block, column):
    return [pl.BlockSpec((TOK, block), lambda i, n, r=r: (r, column(i))) for _, r in sources]


def select_kernel(weighted, parts, numbers, *refs):
    tags, sources, outs, (matrix, scale) = refs[:8], refs[8:16], refs[16:-2], refs[-2:]

    @pl.when(pl.program_id(0) == 0)
    def _():
        experts = [numbers[i].astype(F32) for i in range(4)]
        for s in range(8):
            inside, weight = slot_matrix(tags[s][...], experts)
            matrix[s] = inside.reshape(TOK, TOK).astype(BF16)
            if weighted:
                scale[s] = jnp.sum(
                    (inside * weight[:, None, :]).reshape(TOK, TOK), axis=1, keepdims=True
                )

    for s in range(8):
        rows = jnp.dot(matrix[s], sources[s][...], preferred_element_type=F32)
        if weighted:
            rows = rows * scale[s]
        rows = rows.astype(BF16)
        for i in range(4):
            outs[i % parts][slots_at(s, i, parts), :] = rows[SLOTS * i : SLOTS * (i + 1), :]


def select(numbers, sources, weighted, parts):
    width = sources[0][0].shape[1] - TAGS
    height = 4 * PART // parts
    tags = source_specs(sources, TAGS, lambda i: width // TAGS)
    return pl.pallas_call(
        functools.partial(select_kernel, weighted, parts),
        grid_spec=pltpu.PrefetchScalarGridSpec(
            num_scalar_prefetch=1,
            grid=(width // BLOCK,),
            in_specs=tags + source_specs(sources, BLOCK, lambda i: i),
            out_specs=[pl.BlockSpec((height, BLOCK), lambda i, n: (0, i))] * parts,
            scratch_shapes=[
                pltpu.VMEM((8, TOK, TOK), BF16),
                pltpu.VMEM((8, TOK, 1), F32),
            ],
        ),
        out_shape=[jax.ShapeDtypeStruct((height, width), BF16)] * parts,
        compiler_params=pltpu.CompilerParams(vmem_limit_bytes=VMEM),
        cost_estimate=SHORT,
    )(numbers, *[v for v, _ in sources], *[v for v, _ in sources])


def combine_kernel(weighted, width, parts, numbers, *refs):
    tags, rows, (own, other, matrix) = refs[:8], refs[8:-3], refs[-3:]
    step = pl.program_id(0)

    @pl.when(step == 0)
    def _():
        experts = [numbers[i].astype(F32) for i in range(4)]
        for s in range(8):
            inside, weight = slot_matrix(tags[s][...], experts)
            if weighted:
                inside = inside * weight[:, None, :]
            matrix[s] = inside.reshape(TOK, TOK).T.astype(BF16)

    for s in range(8):
        held = jnp.concatenate(
            [rows[i % parts][slots_at(s, i, parts), :] for i in range(4)], axis=0
        )
        sums = jnp.dot(matrix[s], held, preferred_element_type=F32)
        at = pl.ds(pl.multiple_of(numbers[4 + s // 2] * TOK, TOK), TOK)
        if s % 2 == 0:
            own[at, :] = sums.astype(BF16)
        elif width % BLOCK == 0:
            other[at, :] = sums.astype(BF16)
        else:
            lanes = lax.broadcasted_iota(jnp.int32, sums.shape, 1)
            apart = jnp.where((lanes >= 8) & (lanes < 16), pltpu.roll(sums, 8, 1), 0.0)
            sums = jnp.where(step == width // BLOCK, apart, sums)
            other[at, :] = sums.astype(BF16)


def combine(numbers, sources, rows, weighted):
    width = rows[0].shape[1]
    parts = len(rows)
    tags_at = (sources[0][0].shape[1] - TAGS) // TAGS
    tags = source_specs(sources, TAGS, lambda i: tags_at)
    return pl.pallas_call(
        functools.partial(combine_kernel, weighted, width, parts),
        grid_spec=pltpu.PrefetchScalarGridSpec(
            num_scalar_prefetch=1,
            grid=(pl.cdiv(width, BLOCK),),
            in_specs=tags
            + [pl.BlockSpec((4 * PART // parts, BLOCK), lambda i, n: (0, i))] * parts,
            out_specs=[pl.BlockSpec((4 * TOK, BLOCK), lambda i, n: (0, i))] * 2,
            scratch_shapes=[pltpu.VMEM((8, TOK, TOK), BF16)],
        ),
        compiler_params=pltpu.CompilerParams(vmem_limit_bytes=VMEM),
        out_shape=[jax.ShapeDtypeStruct((4 * TOK, width), BF16)] * 2,
        cost_estimate=SHORT,
    )(numbers, *[v for v, _ in sources], *rows)


def forward_kernel(rows, gate_w, up_w, gate_pre, up_pre, activation):
    gate = dot(rows[...], gate_w[...], ((1,), (0,)))
    up = dot(rows[...], up_w[...], ((1,), (0,)))
    gate_pre[...] = gate
    up_pre[...] = up
    activation[...] = (gate * jax.nn.sigmoid(gate) * up).astype(BF16)


def forward(rows, gate_w, up_w):
    count, width = rows.shape
    hidden = gate_w.shape[1]
    weights = pl.BlockSpec((width, hidden), lambda i: (0, 0))
    block = pl.BlockSpec((PART, hidden), lambda i: (i, 0))
    shapes = [jax.ShapeDtypeStruct((count, hidden), t) for t in (F32, F32, BF16)]
    return pl.pallas_call(
        forward_kernel,
        grid=(count // PART,),
        in_specs=[pl.BlockSpec((PART, width), lambda i: (i, 0)), weights, weights],
        out_specs=[block] * 3,
        out_shape=shapes,
        compiler_params=pltpu.CompilerParams(vmem_limit_bytes=VMEM),
        cost_estimate=SHORT,
    )(rows, gate_w, up_w)


def out_kernel(activation, down_w, out):
    out[...] = dot(activation[...], down_w[...], ((1,), (0,))).astype(BF16)


def expert_output(activation, down_w):
    count, hidden = activation.shape
    width = down_w.shape[1]
    return pl.pallas_call(
        out_kernel,
        grid=(count // PART,),
        in_specs=[
            pl.BlockSpec((PART, hidden), lambda i: (i, 0)),
            pl.BlockSpec((hidden, width), lambda i: (0, 0)),
        ],
        out_specs=pl.BlockSpec((PART, width), lambda i: (i, 0)),
        out_shape=jax.ShapeDtypeStruct((count, width), BF16),
        compiler_params=pltpu.CompilerParams(vmem_limit_bytes=VMEM),
        cost_estimate=SHORT,
    )(activation, down_w)


def backward_kernel(g0, g1, g2, g3, down_w, gate_pre, up_pre, activation, *refs):
    gate_grad, up_grad, slots, down_part = refs
    grads, run = (g0, g1, g2, g3), C * SLOTS
    act = activation[...]
    down = None
    act_grads = []
    for j in range(4):
        act_grads.append(dot(grads[j][...], down_w[...], ((1,), (1,))))
        turned_act = jnp.concatenate(
            [act[(4 * k + j) * run : (4 * k + j + 1) * run] for k in range(4)], axis=0
        )
        term = dot(turned_act, grads[j][...], ((0,), (0,)))
        down = term if down is None else down + term
    down_part[...] = down.astype(BF16)
    for k in range(4):
        at = slice(k * PART, (k + 1) * PART)
        act_grad = jnp.concatenate(
            [act_grads[j][k * run : (k + 1) * run] for j in range(4)], axis=0
        )
        gate, up = gate_pre[at, :], up_pre[at, :]
        sigmoid = jax.nn.sigmoid(gate)
        gate_grad[at, :] = (act_grad * up * sigmoid * (1.0 + gate * (1.0 - sigmoid))).astype(BF16)
        up_grad[at, :] = (act_grad * gate * sigmoid).astype(BF16)
        term = jnp.sum(act[at].astype(F32) * act_grad, axis=1, keepdims=True)

        @pl.when(pl.program_id(0) == 0)
        def _(at=at, term=term):
            slots[at, :] = term

        @pl.when(pl.program_id(0) > 0)
        def _(at=at, term=term):
            slots[at, :] += term


def backward(grads, down_w, gate_pre, up_pre, activation):
    hidden, width = down_w.shape
    count, step = activation.shape[0], 256
    column = pl.BlockSpec((count, step), lambda i: (0, i))
    weights = pl.BlockSpec((step, width), lambda i: (i, 0))
    return pl.pallas_call(
        backward_kernel,
        grid=(hidden // step,),
        in_specs=[pl.BlockSpec((PART, width), lambda i: (0, 0))] * 4 + [weights] + [column] * 3,
        out_specs=[column, column, pl.BlockSpec((count, 1), lambda i: (0, 0)), weights],
        out_shape=[
            jax.ShapeDtypeStruct((count, hidden), BF16),
            jax.ShapeDtypeStruct((count, hidden), BF16),
            jax.ShapeDtypeStruct((count, 1), F32),
            jax.ShapeDtypeStruct((hidden, width), BF16),
        ],
        compiler_params=pltpu.CompilerParams(vmem_limit_bytes=VMEM),
        cost_estimate=SHORT,
    )(*grads, down_w, gate_pre, up_pre, activation)


def part_kernel(rows, grad, out):
    out[...] = dot(rows[...], grad[...], ((0,), (0,))).astype(BF16)


def weight_part(rows, grad):
    count, width = rows.shape
    hidden = grad.shape[1]
    return pl.pallas_call(
        part_kernel,
        grid=(width // BLOCK,),
        in_specs=[
            pl.BlockSpec((count, BLOCK), lambda i: (0, i)),
            pl.BlockSpec((count, hidden), lambda i: (0, 0)),
        ],
        out_specs=pl.BlockSpec((BLOCK, hidden), lambda i: (i, 0)),
        out_shape=jax.ShapeDtypeStruct((width, hidden), BF16),
        compiler_params=pltpu.CompilerParams(vmem_limit_bytes=VMEM),
        cost_estimate=SHORT,
    )(rows, grad)


def row_kernel(steps, gate_grad, up_grad, gate_w, up_w, high, low, *outs):
    step = pl.program_id(0)

    def put(rows):
        for k in range(4):
            for j in range(4):
                at = (k * 4 + j) * C * SLOTS
                outs[j][k * C * SLOTS : (k + 1) * C * SLOTS, :] = rows(j, at, at + C * SLOTS)

    @pl.when(step < steps)
    def _():
        wide = dot(gate_grad[...], gate_w[...], ((1,), (1,)))
        wide = (wide + dot(up_grad[...], up_w[...], ((1,), (1,)))).astype(BF16)
        put(lambda j, a, b: wide[a:b])

    @pl.when(step == steps)
    def _():
        lanes = lax.broadcasted_iota(jnp.int32, (C * SLOTS, BLOCK), 1)

        def rows(j, a, b):
            upper = jnp.where(lanes == j, high[a:b].astype(F32), 0.0)
            return jnp.where(lanes == 4 + j, low[a:b].astype(F32), upper).astype(BF16)

        put(rows)


def row_gradients(gate_grad, up_grad, gate_w, up_w, high, low):
    width, hidden = gate_w.shape
    steps = width // BLOCK
    whole = pl.BlockSpec(gate_grad.shape, lambda i: (0, 0))
    weights = pl.BlockSpec((BLOCK, hidden), lambda i: (jnp.minimum(i, steps - 1), 0))
    column = pl.BlockSpec(high.shape, lambda i: (0, 0))
    return pl.pallas_call(
        functools.partial(row_kernel, steps),
        grid=(steps + 1,),
        in_specs=[whole, whole, weights, weights, column, column],
        out_specs=[pl.BlockSpec((8 * SLOTS, BLOCK), lambda i: (0, i))] * 4,
        out_shape=[jax.ShapeDtypeStruct((8 * SLOTS, width + TAGS), BF16)] * 4,
        compiler_params=pltpu.CompilerParams(vmem_limit_bytes=VMEM),
        cost_estimate=SHORT,
    )(gate_grad, up_grad, gate_w, up_w, high, low)


def dot(a, b, contract):
    return lax.dot_general(a, b, (contract, ((), ())), preferred_element_type=F32)


def after(value, *earlier):
    return lax.optimization_barrier((value, earlier))[0]


def halves(value):
    high = value.astype(BF16)
    return high, (value - high.astype(F32)).astype(BF16)


def core_sum(parts):
    own, other = parts
    return (own.astype(F32) + moved(other, dc=1).astype(F32)).astype(BF16)


def after(value, *earlier):
    return lax.optimization_barrier((value, earlier))[0]


def halves(value):
    high = value.astype(BF16)
    return high, (value - high.astype(F32)).astype(BF16)


def core_sum(parts):
    own, other = parts
    return (own.astype(F32) + moved(other, dc=1).astype(F32)).astype(BF16)


def home(sums, axis):
    return [along(v, axis, -i).astype(F32) for i, v in enumerate(sums)]


def local(tokens, expert_ids, combine_weights, grad_output, swap_flags, w_gate, w_up, w_down):
    width = tokens.shape[1]
    me = lax.axis_index("expert")
    z, x, c = me // (X * C), me // C % X, me % C
    gate_w, up_w, down_w = w_gate[0], w_up[0], w_down[0]
    high, low = halves(combine_weights)
    tags = jnp.concatenate(
        [expert_ids.astype(BF16), high, low, jnp.zeros((TOK, TAGS - 24), BF16)], axis=1
    )

    along_x = [[place(i, j, k) for j in range(X)] for i in range(Z) for k in range(C)]
    along_z = [[place(i, j, k) for i in range(Z)] for j in range(X) for k in range(C)]

    def exchanged(v, groups=along_x):
        parts = v.reshape(4, -1, v.shape[1])
        parts = lax.all_to_all(parts, "expert", 0, 0, axis_index_groups=groups, tiled=True)
        return parts.reshape(v.shape)

    tagged = jnp.concatenate([tokens, tags], axis=1)
    legs = [along(tagged, "z", j) for j in range(4)]
    token_parts = [(v, 0) for part in legs for v in (part, moved(part, dc=1))]
    tagged = jnp.concatenate([grad_output, tags], axis=1)
    gathered = exchanged(jnp.concatenate([tagged] * X, axis=0))
    arrived = moved(gathered, dc=1)
    cotangent_parts = [(v, i) for i in range(X) for v in (gathered, arrived)]
    by_x = jnp.stack(
        [place(z, i, c) for i in range(X)] + [(z - j) % Z for j in range(4)]
    ).astype(jnp.int32)
    by_z = jnp.stack(
        [place(z + j, x, c) for j in range(4)] + [(x - i) % X for i in range(X)]
    ).astype(jnp.int32)

    rows = exchanged(select(by_x, token_parts, False, 1)[0])
    sent = select(by_z, cotangent_parts, True, 4)
    grads = [along(v, "z", j) for j, v in enumerate(sent)]

    gate_pre, up_pre, activation = forward(rows, gate_w, up_w)
    expert_out = expert_output(activation, down_w)
    back = exchanged(expert_out)
    gate_grad, up_grad, weight_slots, down_part = backward(
        grads, down_w, gate_pre, up_pre, after(activation, expert_out)
    )
    gate_part = weight_part(rows, gate_grad)
    gate_grad, up_grad, weight_slots = after((gate_grad, up_grad, weight_slots), gate_part)
    back_grads = row_gradients(gate_grad, up_grad, gate_w, up_w, *halves(weight_slots))
    back_grads = [along(v, "z", -j) for j, v in enumerate(back_grads)]
    numbers = jnp.arange(EXPERTS, dtype=jnp.int32)
    my_flag = jnp.sum(jnp.where(numbers == me, swap_flags, 0))

    def with_partners(mine):
        return mine, moved(mine, dz=Z // 2)

    def traded(pair):
        return jnp.where(my_flag == 1, pair[1], pair[0]).astype(F32)[None]

    down_pair = with_partners(lax.psum_scatter(down_part, "dp", scatter_dimension=1, tiled=True))
    up_part = weight_part(rows, after(up_grad, back_grads))
    gate_pair = with_partners(lax.psum_scatter(gate_part, "dp", scatter_dimension=0, tiled=True))
    up_pair = with_partners(lax.psum_scatter(up_part, "dp", scatter_dimension=0, tiled=True))

    token_sums = combine(by_x, token_parts, [back], True)
    token_sums = core_sum(token_sums)
    cotangent_sums = core_sum(combine(after(by_z, token_sums, up_part), cotangent_parts, back_grads, False))
    arrived = exchanged(token_sums, along_z).reshape(Z, TOK, width)
    mixed = jnp.sum(arrived.astype(F32), axis=0).astype(BF16)
    cotangent_sums = after(cotangent_sums, token_sums)
    parts = [
        along(cotangent_sums[TOK * k : TOK * (k + 1)], "x", -k).astype(F32) for k in range(4)
    ]
    grad_tokens = sum(v[:, :width] for v in parts).astype(BF16)
    down_sum = traded(down_pair)
    gate_sum, up_sum = [traded(after(v, token_sums, cotangent_sums)) for v in (gate_pair, up_pair)]
    of_expert = jnp.concatenate([v[:, width : width + 16] for v in parts], axis=1)
    expert_at = jnp.stack(
        [place(z + j, x + k, c ^ b) for k in range(4) for b in range(C) for _ in range(2) for j in range(4)]
    )
    grad_weights = (
        jnp.sum(
            jnp.where(expert_ids[:, :, None] == expert_at, of_expert[:, None, :], 0.0), axis=2
        )
        / combine_weights
    )

    return (mixed, grad_tokens, grad_weights, gate_sum, up_sum, down_sum)


def solution(mesh):
    return jax.shard_map(
        local,
        mesh=mesh,
        in_specs=(
            P(("expert", "dp"), None),
            P(("expert", "dp"), None),
            P(("expert", "dp"), None),
            P(("expert", "dp"), None),
            P(),
            P("expert", None, None),
            P("expert", None, None),
            P("expert", None, None),
        ),
        out_specs=(
            P(("expert", "dp"), None),
            P(("expert", "dp"), None),
            P(("expert", "dp"), None),
            P("expert", "dp", None),
            P("expert", "dp", None),
            P("expert", None, "dp"),
        ),
        check_vma=False,
    )
```
